256 devices in a mesh: dp: 16 (over y, z_lo, core), tensor: 16 (over z_hi, x).
Axes of the slice: x: 4, y: 4, z: 8 (z_hi: 4, z_lo: 2; z = z_hi * 2 + z_lo), core: 2. Of those that a mesh axis runs over, the one named last changes fastest.
Arguments:
- normed: bfloat16 [18432, 1536], P(('dp', 'tensor')), may hold values from -24 to 24
- out_grad: bfloat16 [18432, 1536], P(('dp', 'tensor')), may hold values from -24 to 24
- gate_weight: bfloat16 [1536, 8960], P(None, 'tensor'), may hold values from -0.15625 to 0.15625
- up_weight: bfloat16 [1536, 8960], P(None, 'tensor'), may hold values from -0.15625 to 0.15625
- down_weight: bfloat16 [8960, 1536], P('tensor'), may hold values from -0.0625 to 0.0625
Outputs:
- grad_input: bfloat16 [18432, 1536], P(('dp', 'tensor'))
- grad_gate: float32 [1536, 8960], P('dp', 'tensor')
- grad_up: float32 [1536, 8960], P('dp', 'tensor')
- grad_down: float32 [8960, 1536], P('tensor', 'dp')
The draws below stay inside these ranges and needn't reach their ends.
All inputs are finite; a program needn't handle non-finite values.
Results may differ from the reference program's by a relative error of at most 0.0049.
Values may be sent and summed in bfloat16 or wider, within the bound.
No kernel may reach another device: no remote copies, remote signals or barrier semaphores. Data moves between devices by JAX's collectives and lax.ppermute only.
A program may use at most 128 MiB of HBM per device.

```python
import jax
import jax.numpy as jnp
from jax import lax

D = 1536
FF = 8960
TOK_DEV = 72
TOKENS = 18432
N_DP = 16
N_TENSOR = 16


def strengthened(drawn, rng, source, target, blocks, factor):
    owner, partner = [(jnp.arange(drawn.shape[axis_at]) // (drawn.shape[axis_at] // blocks)).reshape([-1 if axis == axis_at else 1 for axis in range(drawn.ndim)]) for axis_at in (source, target)]
    chosen = jax.random.permutation(rng, blocks)[partner]
    strong = (owner == chosen) | (owner == (partner + blocks // 2) % blocks)
    return jnp.where(strong, factor * drawn, drawn)


def block_levels(key, extent, cuts, smallest, largest):
    def one(position, parts):
        heights = jax.random.uniform(jax.random.fold_in(jax.random.fold_in(key, 6), position), (parts,), jnp.float32, smallest / len(cuts), largest / len(cuts))
        return jnp.repeat(jnp.exp(heights), extent[position] // parts).reshape((-1,) + (1,) * (len(extent) - position - 1))

    loudness = one(*cuts[0])
    for cut in cuts[1:]:
        loudness = loudness * one(*cut)
    return loudness


def bell_draw(own_key, dims, scale, bound, shards=(), dtype=jnp.bfloat16):
    drawn = jax.random.normal(own_key, dims, jnp.float32) * scale
    if len(shards) > 0:
        drawn = block_levels(own_key, dims, shards, -0.22, 0.18) * drawn
    return jnp.clip(drawn, min=-bound, max=bound).astype(dtype)


def gaussian_with(key, dims, spread, bound, split, heavy, held_as=jnp.bfloat16):
    result = spread * jax.random.normal(key, dims, jnp.float32)
    if split:
        result = result * block_levels(key, dims, split, -0.22, 0.18)
    return jnp.clip(strengthened(result, jax.random.fold_in(key, 3), *heavy), -bound, bound).astype(held_as)


def setup_inputs(seed: int = 0) -> dict:
    key_list = jax.random.split(jax.random.key(seed), 6)
    normed = gaussian_with(key_list[0], (TOKENS, D), 1.0, 24.0, ((0, 256),), (0, 1, 256, 6.0))
    out_grad = gaussian_with(key_list[1], (TOKENS, D), 1.0, 24.0, ((0, 256),), (0, 1, 256, 6.0))
    gate_weight = bell_draw(key_list[2], (D, FF), D ** -0.5, 0.15625, ((1, 16),))
    up_weight = bell_draw(key_list[3], (D, FF), D ** -0.5, 0.15625, ((1, 16),))
    down_weight = bell_draw(key_list[4], (FF, D), FF ** -0.5, 0.0625, ((0, 16),))
    return {"normed": normed, "out_grad": out_grad, "gate_weight": gate_weight, "up_weight": up_weight, "down_weight": down_weight}


def contract(left, right, left_dim, right_dim):
    return lax.dot_general(left, right, (((left_dim,), (right_dim,)), ((), ())), preferred_element_type=jnp.float32)


def reference(normed, out_grad, gate_weight, up_weight, down_weight):
    window = TOK_DEV * N_TENSOR
    inputs = normed.reshape(N_DP, window, D)
    grads = out_grad.reshape(N_DP, window, D)

    def one_window(carry, pair):
        rows, upstream = pair
        gate = jnp.dot(rows, gate_weight, preferred_element_type=jnp.float32)
        up = jnp.dot(rows, up_weight, preferred_element_type=jnp.float32)
        sig = jax.nn.sigmoid(gate)
        act = gate * sig
        hidden = (act * up).astype(jnp.bfloat16)
        dhidden = contract(upstream, down_weight, 1, 1)
        dgate = (dhidden * up * sig * (1.0 + gate * (1.0 - sig))).astype(jnp.bfloat16)
        dup = (dhidden * act).astype(jnp.bfloat16)
        grad_rows = (contract(dgate, gate_weight, 1, 1) + contract(dup, up_weight, 1, 1)).astype(jnp.bfloat16)
        sum_gate = carry[0] + contract(rows, dgate, 0, 0)
        sum_up = carry[1] + contract(rows, dup, 0, 0)
        sum_down = carry[2] + contract(hidden, upstream, 0, 0)
        return (sum_gate, sum_up, sum_down), grad_rows

    start = (jnp.zeros((D, FF), jnp.float32), jnp.zeros((D, FF), jnp.float32), jnp.zeros((FF, D), jnp.float32))
    sums, grad_rows = lax.scan(one_window, start, (inputs, grads))
    return (grad_rows.reshape(TOKENS, D), sums[0] / N_DP, sums[1] / N_DP, sums[2] / N_DP)
```

```python
import functools

import jax
import jax.numpy as jnp
from jax import lax
from jax.experimental import pallas as pl
from jax.experimental.pallas import tpu as pltpu
from jax.sharding import PartitionSpec as P

F32, BF16 = jnp.float32, jnp.bfloat16
VMEM = pl.BlockSpec(memory_space=pltpu.VMEM)
LIMIT = 40 << 20


def contract(left, right, left_dim, right_dim):
    return lax.dot_general(
        left, right, (((left_dim,), (right_dim,)), ((), ())), preferred_element_type=F32
    )


def along_x(value, step):
    return lax.ppermute(value, "tensor", [(i, i // 4 * 4 + (i + step) % 4) for i in range(16)])


def along_z(value, step):
    return lax.ppermute(value, "tensor", [(i, (i + 4 * step) % 16) for i in range(16)])


def along_y(value, step):
    return lax.ppermute(value, "dp", [(i, (i + 4 * step) % 16) for i in range(16)])


def other_z_lo(value):
    return lax.ppermute(value, "dp", [(i, i ^ 2) for i in range(16)])


def other_core(value):
    return lax.ppermute(value, "dp", [(i, i ^ 1) for i in range(16)])


def stage_body(groups, *refs):
    blocks, (weight, down), outs = refs[: 4 * groups], refs[4 * groups : 4 * groups + 2], refs[4 * groups + 2 :]
    rows_out, grads_out, both_out, hidden_out, own_out = outs[:5]
    tokens, hidden_units = blocks[0].shape[1], down.shape[0]
    for i, block in enumerate(blocks):
        rows_out[i * tokens : (i + 1) * tokens, :] = block[0]
        grads_out[i * tokens : (i + 1) * tokens, :] = block[1]
    for g in range(groups):
        part_of = pl.ds(g * 4 * tokens, 4 * tokens)
        gate_up = jnp.dot(rows_out[part_of, :], weight[...], preferred_element_type=F32)
        part = contract(grads_out[part_of, :], down[...], 1, 1)
        gate, up = gate_up[:, :hidden_units], gate_up[:, hidden_units:]
        sig = jax.nn.sigmoid(gate)
        act = gate * sig
        hidden_out[part_of, :] = (act * up).astype(BF16)
        dgate = (part * up * sig * (1.0 + gate * (1.0 - sig))).astype(BF16)
        dup = (part * act).astype(BF16)
        both = jnp.concatenate((dgate, dup), axis=1)
        both_out[part_of, :] = both
        grad = contract(both, weight[...], 1, 1)
        own_out[g] = grad[:tokens]
        for i in range(1, 4):
            outs[4 + i][g] = grad[i * tokens : (i + 1) * tokens].astype(BF16)


def stage(blocks, weight, down):
    groups = len(blocks) // 4
    tokens, model = blocks[0].shape[1:]
    hidden_units = down.shape[0]
    m = len(blocks) * tokens
    shape = jax.ShapeDtypeStruct
    outs = [shape((m, model), BF16)] * 2 + [shape((m, 2 * hidden_units), BF16), shape((m, hidden_units), BF16)]
    outs += [shape((groups, tokens, model), F32)] + [shape((groups, tokens, model), BF16)] * 3
    return pl.pallas_call(
        functools.partial(stage_body, groups),
        out_shape=outs,
        in_specs=[VMEM] * (len(blocks) + 2),
        out_specs=[VMEM] * 8,
        compiler_params=pltpu.CompilerParams(vmem_limit_bytes=LIMIT),
        cost_estimate=pl.CostEstimate(
            flops=10 * m * model * hidden_units, bytes_accessed=groups * (6 << 20), transcendentals=m * hidden_units
        ),
        name="stage",
    )(*blocks, weight, down)


def weight_body(has_total, last, place, *refs):
    left, right = refs[0], refs[1]
    total = contract(left[...], right[...], 0, 0)
    if has_total:
        total = total + refs[2][...]
    outs = refs[2 + has_total :]
    if not last:
        outs[0][...] = total
        return
    send, keep, held = outs
    core, part = place[1], keep.shape[2]
    held[...] = total
    for z in range(2):
        mine = pl.ds(pl.multiple_of(z * 2 * part + core * part, 32), part)
        others = pl.ds(pl.multiple_of(z * 2 * part + (1 - core) * part, 32), part)
        keep[0, z] = held[mine, :]
        send[0, z] = held[others, :].astype(BF16)


def weight_grad(place, left, right, total, last):
    m, model = left.shape
    n = right.shape[1]
    chunk, part = model // 4, model // 16
    shape = jax.ShapeDtypeStruct

    def at(r, place):
        return lax.rem(place[0] + r, 4)

    in_specs = [
        pl.BlockSpec((m, chunk), lambda r, place: (0, at(r, place))),
        pl.BlockSpec((m, n), lambda r, place: (0, 0)),
    ]
    args = [left, right]
    if total is not None:
        in_specs.append(pl.BlockSpec((chunk, n), lambda r, place: (at(r, place), 0)))
        args.append(total)
    if last:
        out_specs = [pl.BlockSpec((1, 2, part, n), lambda r, place: (r, 0, 0, 0))] * 2
        out_shape = [shape((4, 2, part, n), BF16), shape((4, 2, part, n), F32)]
        scratch = [pltpu.VMEM((chunk, n), F32)]
    else:
        out_specs = [pl.BlockSpec((chunk, n), lambda r, place: (at(r, place), 0))]
        out_shape = [shape((model, n), F32)]
        scratch = []
    return pl.pallas_call(
        functools.partial(weight_body, int(total is not None), last),
        grid_spec=pltpu.PrefetchScalarGridSpec(
            num_scalar_prefetch=1, grid=(4,), in_specs=in_specs, out_specs=out_specs, scratch_shapes=scratch
        ),
        out_shape=out_shape,
        compiler_params=pltpu.CompilerParams(vmem_limit_bytes=LIMIT),
        cost_estimate=pl.CostEstimate(flops=4 * m * model * n, bytes_accessed=8 * model * n, transcendentals=0),
        name="weight_grad",
    )(place, *args)


def over_replicas(send, keep, z_lo):
    got = other_core(send)
    sums = [keep[r] + got[r].astype(F32) for r in range(4)]
    one = along_y(sums[1].astype(BF16), 1)
    three = along_y(sums[3].astype(BF16), -1)
    two = along_y(sums[2].astype(BF16), 2)
    total = sums[0] + one.astype(F32) + three.astype(F32) + two.astype(F32)
    mine = lax.dynamic_index_in_dim(total, z_lo, 0, keepdims=False)
    others = lax.dynamic_index_in_dim(total, 1 - z_lo, 0, keepdims=False).astype(BF16)
    return mine + other_z_lo(others).astype(F32)


def gather_x(block):
    left, right, far = along_x(block, 1), along_x(block, -1), along_x(block, 2)
    return [block, left, right, far]


def scatter_x(own, to_left, to_right, to_far):
    got = along_x(to_left, -1), along_x(to_right, 1), along_x(to_far, 2)
    return own + got[0].astype(F32) + got[1].astype(F32) + got[2].astype(F32)


def on_device(normed, out_grad, gate_weight, up_weight, down_weight):
    replicas = lax.axis_size("dp")
    dp = lax.axis_index("dp")
    place = jnp.stack((dp // 4, dp % 2)).astype(jnp.int32)
    z_lo = dp // 2 % 2
    weight = jnp.concatenate((gate_weight, up_weight), axis=1)
    own = jnp.stack((normed, out_grad))

    below, above = along_z(own, 1), along_z(own, -1)
    home = gather_x(own)
    far = along_z(own, 2)
    b_left, b_right = along_x(below, 1), along_x(below, -1)
    a_left, a_right = along_x(above, 1), along_x(above, -1)
    b_far, a_far = along_x(b_left, 1), along_x(a_right, -1)
    near = [below, b_left, b_right, b_far, above, a_left, a_right, a_far]
    away = gather_x(far)

    home = stage(home, weight, down_weight)
    pair, down = weight_grad(place, home[0], home[2], None, False), weight_grad(place, home[1], home[3], None, False)
    near = stage(near, weight, down_weight)
    pair = weight_grad(place, near[0], near[2], pair[0], False)
    down = weight_grad(place, near[1], near[3], down[0], False)
    away = stage(away, weight, down_weight)
    down = weight_grad(place, away[1], away[3], down[0], True)
    pair = weight_grad(place, away[0], away[2], pair[0], True)

    near = scatter_x(*near[4:])
    from_below = along_z(near[1].astype(BF16), 1)
    from_above = along_z(near[0].astype(BF16), -1)
    away = scatter_x(*away[4:])
    from_far = along_z(away[0].astype(BF16), 2)
    home = scatter_x(*home[4:])
    grad_input = home[0] + from_below.astype(F32) + from_above.astype(F32) + from_far.astype(F32)

    grad_down = over_replicas(*down, z_lo) / replicas
    grad_pair = over_replicas(*pair, z_lo) / replicas
    half = gate_weight.shape[1]
    return grad_input.astype(BF16), grad_pair[:, :half], grad_pair[:, half:], grad_down.T


def solution(mesh):
    return jax.shard_map(
        on_device,
        mesh=mesh,
        in_specs=(
            P(("dp", "tensor"), None),
            P(("dp", "tensor"), None),
            P(None, "tensor"),
            P(None, "tensor"),
            P("tensor", None),
        ),
        out_specs=(
            P(("dp", "tensor"), None),
            P("dp", "tensor"),
            P("dp", "tensor"),
            P("tensor", "dp"),
        ),
        check_vma=False,
    )
```

```python
import functools

import jax
import jax.numpy as jnp
from jax import lax
from jax.experimental import pallas as pl
from jax.experimental.pallas import tpu as pltpu
from jax.sharding import PartitionSpec as P

F32, BF16 = jnp.float32, jnp.bfloat16
VMEM = pl.BlockSpec(memory_space=pltpu.VMEM)
ANY = pl.BlockSpec(memory_space=pl.ANY)
LIMIT = 40 << 20
SHORT = pl.CostEstimate(flops=0, bytes_accessed=0, transcendentals=0)


def contract(left, right, left_dim, right_dim):
    return lax.dot_general(
        left, right, (((left_dim,), (right_dim,)), ((), ())), preferred_element_type=F32
    )


def along_x(value, step):
    return lax.ppermute(value, "tensor", [(i, i // 4 * 4 + (i + step) % 4) for i in range(16)])


def along_z(value, step):
    return lax.ppermute(value, "tensor", [(i, (i + 4 * step) % 16) for i in range(16)])


def along_y(value, step):
    return lax.ppermute(value, "dp", [(i, (i + 4 * step) % 16) for i in range(16)])


def other_z_lo(value):
    return lax.ppermute(value, "dp", [(i, i ^ 2) for i in range(16)])


def other_core(value):
    return lax.ppermute(value, "dp", [(i, i ^ 1) for i in range(16)])


def pack_body(rows, grads, after, out):
    out[0], out[1] = rows[...], grads[...]


def pack(rows, grads, after):
    return pl.pallas_call(
        pack_body,
        out_shape=jax.ShapeDtypeStruct((2, *rows.shape), rows.dtype),
        in_specs=[VMEM, VMEM, ANY],
        out_specs=VMEM,
        cost_estimate=pl.CostEstimate(flops=0, bytes_accessed=1 << 20, transcendentals=0),
        name="pack",
    )(rows, grads, after)


def partials(both, weight, outs, g):
    tokens = outs[0].shape[1]
    grad = jnp.dot(both, weight[...], preferred_element_type=F32)
    outs[0][g] = grad[:tokens]
    for i in range(1, 4):
        outs[i][g] = grad[i * tokens : (i + 1) * tokens].astype(BF16)


def partial_shapes(groups, tokens, model):
    shape = jax.ShapeDtypeStruct
    return [shape((groups, tokens, model), F32)] + [shape((groups, tokens, model), BF16)] * 3


def stage_body(groups, send, *refs):
    blocks, (weight, down), outs = refs[: 4 * groups], refs[4 * groups : 4 * groups + 2], refs[4 * groups + 2 :]
    rows_out, grads_out, both_out, hidden_out = outs[:4]
    tokens, hidden_units = blocks[0].shape[1], down.shape[0]
    for i, block in enumerate(blocks):
        rows_out[i * tokens : (i + 1) * tokens, :] = block[0]
        grads_out[i * tokens : (i + 1) * tokens, :] = block[1]
    for g in range(groups):
        part_of = pl.ds(g * 4 * tokens, 4 * tokens)
        gate_up = contract(rows_out[part_of, :], weight[...], 1, 1)
        part = contract(grads_out[part_of, :], down[...], 1, 1)
        gate, up = gate_up[:, :hidden_units], gate_up[:, hidden_units:]
        sig = jax.nn.sigmoid(gate)
        act = gate * sig
        hidden_out[part_of, :] = (act * up).astype(BF16)
        dgate = (part * up * sig * (1.0 + gate * (1.0 - sig))).astype(BF16)
        dup = (part * act).astype(BF16)
        both = jnp.concatenate((dgate, dup), axis=1)
        both_out[part_of, :] = both
        if send:
            partials(both, weight, outs[4:], g)


def stage(blocks, weight, down, send):
    groups = len(blocks) // 4
    tokens, model = blocks[0].shape[1:]
    hidden_units = down.shape[0]
    m = len(blocks) * tokens
    shape = jax.ShapeDtypeStruct
    outs = [shape((m, model), BF16)] * 2 + [shape((m, 2 * hidden_units), BF16), shape((m, hidden_units), BF16)]
    if send:
        outs += partial_shapes(groups, tokens, model)
    return pl.pallas_call(
        functools.partial(stage_body, groups, send),
        out_shape=outs,
        in_specs=[VMEM] * (len(blocks) + 2),
        out_specs=[VMEM] * len(outs),
        compiler_params=pltpu.CompilerParams(vmem_limit_bytes=LIMIT),
        cost_estimate=pl.CostEstimate(
            flops=10 * m * model * hidden_units, bytes_accessed=groups * (6 << 20), transcendentals=m * hidden_units
        ),
        name="stage",
    )(*blocks, weight, down)


def late_body(groups, *refs):
    outs = refs[-4:]
    for g in range(groups):
        partials(refs[g][...], refs[groups], outs, g)


def late_partials(both, weight, *after):
    groups, m, model = len(both), both[0].shape[0], weight.shape[1]
    return pl.pallas_call(
        functools.partial(late_body, groups),
        out_shape=partial_shapes(groups, m // 4, model),
        in_specs=[VMEM] * (groups + 1) + [ANY] * len(after),
        out_specs=[VMEM] * 4,
        compiler_params=pltpu.CompilerParams(vmem_limit_bytes=LIMIT),
        cost_estimate=SHORT,
        name="late_partials",
    )(*both, weight, *after)


def weight_body(has_total, n_args, last, place, *refs):
    left, right = refs[0], refs[1]
    total = contract(left[...], right[...], 0, 0)
    if has_total:
        total = total + refs[2][...]
    outs = refs[n_args:]
    if not last:
        outs[0][...] = total
        return
    send, keep, held = outs
    core, part = place[0], keep.shape[2]
    held[...] = total
    for z in range(2):
        mine = pl.ds(pl.multiple_of(z * 2 * part + core * part, 32), part)
        others = pl.ds(pl.multiple_of(z * 2 * part + (1 - core) * part, 32), part)
        keep[0, z] = held[mine, :]
        send[0, z] = held[others, :].astype(BF16)


def weight_grad(place, left, right, total, last, after=None):
    m, model = left.shape
    n = right.shape[1]
    chunk, part = model // 4, model // 16
    shape = jax.ShapeDtypeStruct

    in_specs = [
        pl.BlockSpec((m, chunk), lambda r, place: (0, r)),
        pl.BlockSpec((m, n), lambda r, place: (0, 0)),
    ]
    args = [left, right]
    if total is not None:
        in_specs.append(pl.BlockSpec((chunk, n), lambda r, place: (r, 0)))
        args.append(total)
    if after is not None:
        in_specs.append(ANY)
        args.append(after)
    if last:
        out_specs = [pl.BlockSpec((1, 2, part, n), lambda r, place: (r, 0, 0, 0))] * 2
        out_shape = [shape((4, 2, part, n), BF16), shape((4, 2, part, n), F32)]
        scratch = [pltpu.VMEM((chunk, n), F32)]
    else:
        out_specs = [pl.BlockSpec((chunk, n), lambda r, place: (r, 0))]
        out_shape = [shape((model, n), F32)]
        scratch = []
    return pl.pallas_call(
        functools.partial(weight_body, total is not None, len(args), last),
        grid_spec=pltpu.PrefetchScalarGridSpec(
            num_scalar_prefetch=1, grid=(4,), in_specs=in_specs, out_specs=out_specs, scratch_shapes=scratch
        ),
        out_shape=out_shape,
        compiler_params=pltpu.CompilerParams(vmem_limit_bytes=LIMIT),
        cost_estimate=SHORT if last else pl.CostEstimate(flops=2 * m * model * n, bytes_accessed=8 * model * n, transcendentals=0),
        name="weight_grad",
    )(place, *args)


def add_body(place, got, mine_out, others_out):
    z_lo = place[1]
    for out, z in ((mine_out, z_lo), (others_out, 1 - z_lo)):
        total = got[0, z].astype(F32)
        for y in range(1, 4):
            total = total + got[y, z].astype(F32)
        out[...] = total.astype(out.dtype)


def add_chunks(place, got):
    part, n = got.shape[2:]
    shape = jax.ShapeDtypeStruct
    return pl.pallas_call(
        add_body,
        out_shape=[shape((part, n), F32), shape((part, n), BF16)],
        in_specs=[pl.BlockSpec(memory_space=pltpu.SMEM), VMEM],
        out_specs=[VMEM] * 2,
        compiler_params=pltpu.CompilerParams(vmem_limit_bytes=LIMIT),
        cost_estimate=SHORT,
        name="add_chunks",
    )(place, got)


def cores_body(keep, got, *refs):
    refs[-1][...] = (keep[...] + got[...].astype(F32)).astype(BF16)


def over_cores(send, keep, *after):
    got = other_core(send)
    part, n = keep.shape[2:]
    block = pl.BlockSpec((1, 2, part, n), lambda y: (y, 0, 0, 0))
    return pl.pallas_call(
        cores_body,
        grid=(4,),
        out_shape=jax.ShapeDtypeStruct(keep.shape, BF16),
        in_specs=[block, block] + [ANY] * len(after),
        out_specs=block,
        compiler_params=pltpu.CompilerParams(vmem_limit_bytes=LIMIT),
        cost_estimate=SHORT,
        name="over_cores",
    )(keep, got, *after)


def over_y(sums):
    groups = [[y * 4 + j for y in range(4)] for j in range(4)]
    return lax.all_to_all(sums, "dp", 0, 0, axis_index_groups=groups, tiled=True)


def over_rest(got, place):
    mine, others = add_chunks(place, got)
    return mine + other_z_lo(others).astype(F32)


def add_parts_body(groups, own, left, right, far, *refs):
    for g, out in enumerate(refs[-groups:]):
        total = own[g] + left[g].astype(F32) + right[g].astype(F32) + far[g].astype(F32)
        out[...] = total.astype(out.dtype)


def scatter_x(own, to_left, to_right, to_far, types, *after):
    got = along_x(to_left, -1), along_x(to_right, 1), along_x(to_far, 2)
    return pl.pallas_call(
        functools.partial(add_parts_body, len(types)),
        out_shape=[jax.ShapeDtypeStruct(own.shape[1:], kind) for kind in types],
        in_specs=[VMEM] * 4 + [ANY] * len(after),
        out_specs=[VMEM] * len(types),
        compiler_params=pltpu.CompilerParams(vmem_limit_bytes=LIMIT),
        cost_estimate=SHORT,
        name="add_parts",
    )(own, *got, *after)


def on_device(normed, out_grad, gate_weight, up_weight, down_weight):
    replicas = lax.axis_size("dp")
    dp = lax.axis_index("dp")
    place = jnp.stack((dp % 2, dp // 2 % 2)).astype(jnp.int32)
    weight = jnp.concatenate((gate_weight.T, up_weight.T), axis=0)
    own = jnp.stack((normed, out_grad))

    below, above = along_z(own, 1), along_z(own, -1)
    left, right = along_x(own, 1), along_x(own, -1)
    again = pack(normed, out_grad, left)
    home = [own, left, right, along_x(again, 2)]
    far = along_z(again, 2)
    b_left, b_right = along_x(below, 1), along_x(below, -1)
    a_left, a_right = along_x(above, 1), along_x(above, -1)
    b_far, a_far = along_x(b_left, 1), along_x(a_right, -1)
    near = [below, b_left, b_right, b_far, above, a_left, a_right, a_far]
    away = [far, along_x(far, 1), along_x(far, -1), along_x(far, 2)]

    home = stage(home, weight, down_weight, False)
    pair, down = weight_grad(place, home[0], home[2], None, False), weight_grad(place, home[1], home[3], None, False)
    near = stage(near, weight, down_weight, True)
    pair = weight_grad(place, near[0], near[2], pair[0], False)
    down = weight_grad(place, near[1], near[3], down[0], False)
    away = stage(away, weight, down_weight, False)
    pair = weight_grad(place, away[0], away[2], pair[0], True)
    late = late_partials([away[2], home[2]], weight, pair[0])
    pair = over_cores(*pair, late[0])
    down = weight_grad(place, away[1], away[3], down[0], True, pair)
    below, above = scatter_x(*near[4:], (BF16, BF16), down[0])
    from_below, from_above = along_z(above, 1), along_z(below, -1)
    pair = over_y(pair)
    down = over_cores(*down, pair)
    far, mine = scatter_x(*late, (BF16, F32), below)
    down = over_y(down)
    from_far = along_z(far, 2)
    grad_input = mine + from_below.astype(F32) + from_above.astype(F32) + from_far.astype(F32)

    grad_pair = over_rest(pair, place) / replicas
    grad_down = over_rest(down, place) / replicas
    half = gate_weight.shape[1]
    return grad_input.astype(BF16), grad_pair[:, :half], grad_pair[:, half:], grad_down.T


def solution(mesh):
    return jax.shard_map(
        on_device,
        mesh=mesh,
        in_specs=(
            P(("dp", "tensor"), None),
            P(("dp", "tensor"), None),
            P(None, "tensor"),
            P(None, "tensor"),
            P("tensor", None),
        ),
        out_specs=(
            P(("dp", "tensor"), None),
            P("dp", "tensor"),
            P("dp", "tensor"),
            P("tensor", "dp"),
        ),
        check_vma=False,
    )
```

```python
import functools

import jax
import jax.numpy as jnp
from jax import lax
from jax.experimental import pallas as pl
from jax.experimental.pallas import tpu as pltpu
from jax.sharding import PartitionSpec as P

F32, BF16 = jnp.float32, jnp.bfloat16
VMEM = pl.BlockSpec(memory_space=pltpu.VMEM)
ANY = pl.BlockSpec(memory_space=pl.ANY)
LIMIT = 40 << 20
SHORT = pl.CostEstimate(flops=0, bytes_accessed=0, transcendentals=0)


def contract(left, right, left_dim, right_dim):
    return lax.dot_general(
        left, right, (((left_dim,), (right_dim,)), ((), ())), preferred_element_type=F32
    )


def along_x(value, step):
    return lax.ppermute(value, "tensor", [(i, i // 4 * 4 + (i + step) % 4) for i in range(16)])


def along_z(value, step):
    return lax.ppermute(value, "tensor", [(i, (i + 4 * step) % 16) for i in range(16)])


def along_y(value, step):
    return lax.ppermute(value, "dp", [(i, (i + 4 * step) % 16) for i in range(16)])


def other_z_lo(value):
    return lax.ppermute(value, "dp", [(i, i ^ 2) for i in range(16)])


def other_core(value):
    return lax.ppermute(value, "dp", [(i, i ^ 1) for i in range(16)])


def pack_body(rows, grads, after, out):
    out[0], out[1] = rows[...], grads[...]


def pack(rows, grads, after):
    return pl.pallas_call(
        pack_body,
        out_shape=jax.ShapeDtypeStruct((2, *rows.shape), rows.dtype),
        in_specs=[VMEM, VMEM, ANY],
        out_specs=VMEM,
        cost_estimate=pl.CostEstimate(flops=0, bytes_accessed=1 << 20, transcendentals=0),
        name="pack",
    )(rows, grads, after)


def partials(both, weight, outs, g):
    tokens = outs[0].shape[1]
    grad = jnp.dot(both, weight[...], preferred_element_type=F32)
    outs[0][g] = grad[:tokens]
    for i in range(1, 4):
        outs[i][g] = grad[i * tokens : (i + 1) * tokens].astype(BF16)


def partial_shapes(groups, tokens, model):
    shape = jax.ShapeDtypeStruct
    return [shape((groups, tokens, model), F32)] + [shape((groups, tokens, model), BF16)] * 3


def stage_body(groups, send, *refs):
    blocks, (weight, down), outs = refs[: 4 * groups], refs[4 * groups : 4 * groups + 2], refs[4 * groups + 2 :]
    rows_out, grads_out, both_out, hidden_out = outs[:4]
    tokens, hidden_units = blocks[0].shape[1], down.shape[0]
    for i, block in enumerate(blocks):
        rows_out[i * tokens : (i + 1) * tokens, :] = block[0]
        grads_out[i * tokens : (i + 1) * tokens, :] = block[1]
    for g in range(groups):
        part_of = pl.ds(g * 4 * tokens, 4 * tokens)
        gate_up = contract(rows_out[part_of, :], weight[...], 1, 1)
        part = contract(grads_out[part_of, :], down[...], 1, 1)
        gate, up = gate_up[:, :hidden_units], gate_up[:, hidden_units:]
        sig = jax.nn.sigmoid(gate)
        act = gate * sig
        hidden_out[part_of, :] = (act * up).astype(BF16)
        dgate = (part * up * sig * (1.0 + gate * (1.0 - sig))).astype(BF16)
        dup = (part * act).astype(BF16)
        both = jnp.concatenate((dgate, dup), axis=1)
        both_out[part_of, :] = both
        if send:
            partials(both, weight, outs[4:], g)


def stage(blocks, weight, down, send):
    groups = len(blocks) // 4
    tokens, model = blocks[0].shape[1:]
    hidden_units = down.shape[0]
    m = len(blocks) * tokens
    shape = jax.ShapeDtypeStruct
    outs = [shape((m, model), BF16)] * 2 + [shape((m, 2 * hidden_units), BF16), shape((m, hidden_units), BF16)]
    if send:
        outs += partial_shapes(groups, tokens, model)
    return pl.pallas_call(
        functools.partial(stage_body, groups, send),
        out_shape=outs,
        in_specs=[VMEM] * (len(blocks) + 2),
        out_specs=[VMEM] * len(outs),
        compiler_params=pltpu.CompilerParams(vmem_limit_bytes=LIMIT),
        cost_estimate=SHORT if groups == 1 else pl.CostEstimate(
            flops=10 * m * model * hidden_units, bytes_accessed=groups * (6 << 20), transcendentals=m * hidden_units
        ),
        name="stage",
    )(*blocks, weight, down)


def late_body(groups, *refs):
    outs = refs[-4:]
    for g in range(groups):
        partials(refs[g][...], refs[groups], outs, g)


def late_partials(both, weight, *after):
    groups, m, model = len(both), both[0].shape[0], weight.shape[1]
    return pl.pallas_call(
        functools.partial(late_body, groups),
        out_shape=partial_shapes(groups, m // 4, model),
        in_specs=[VMEM] * (groups + 1) + [ANY] * len(after),
        out_specs=[VMEM] * 4,
        compiler_params=pltpu.CompilerParams(vmem_limit_bytes=LIMIT),
        cost_estimate=SHORT,
        name="late_partials",
    )(*both, weight, *after)


def weight_body(has_total, n_args, last, place, *refs):
    left, right = refs[0], refs[1]
    total = contract(left[...], right[...], 0, 0)
    if has_total:
        total = total + refs[2][...]
    outs = refs[n_args:]
    if not last:
        outs[0][...] = total
        return
    send, keep, held = outs
    core, part = place[0], keep.shape[2]
    held[...] = total
    for z in range(2):
        mine = pl.ds(pl.multiple_of(z * 2 * part + core * part, 32), part)
        others = pl.ds(pl.multiple_of(z * 2 * part + (1 - core) * part, 32), part)
        keep[0, z] = held[mine, :]
        send[0, z] = held[others, :].astype(BF16)


def weight_grad(place, left, right, total, last, after=None):
    m, model = left.shape
    n = right.shape[1]
    chunk, part = model // 4, model // 16
    shape = jax.ShapeDtypeStruct

    in_specs = [
        pl.BlockSpec((m, chunk), lambda r, place: (0, r)),
        pl.BlockSpec((m, n), lambda r, place: (0, 0)),
    ]
    args = [left, right]
    if total is not None:
        in_specs.append(pl.BlockSpec((chunk, n), lambda r, place: (r, 0)))
        args.append(total)
    if after is not None:
        in_specs.append(ANY)
        args.append(after)
    if last:
        out_specs = [pl.BlockSpec((1, 2, part, n), lambda r, place: (r, 0, 0, 0))] * 2
        out_shape = [shape((4, 2, part, n), BF16), shape((4, 2, part, n), F32)]
        scratch = [pltpu.VMEM((chunk, n), F32)]
    else:
        out_specs = [pl.BlockSpec((chunk, n), lambda r, place: (r, 0))]
        out_shape = [shape((model, n), F32)]
        scratch = []
    return pl.pallas_call(
        functools.partial(weight_body, total is not None, len(args), last),
        grid_spec=pltpu.PrefetchScalarGridSpec(
            num_scalar_prefetch=1, grid=(4,), in_specs=in_specs, out_specs=out_specs, scratch_shapes=scratch
        ),
        out_shape=out_shape,
        compiler_params=pltpu.CompilerParams(vmem_limit_bytes=LIMIT),
        cost_estimate=SHORT if last or total is None else pl.CostEstimate(flops=2 * m * model * n, bytes_accessed=8 * model * n, transcendentals=0),
        name="weight_grad",
    )(place, *args)


def add_body(place, got, mine_out, others_out):
    z_lo = place[1]
    for out, z in ((mine_out, z_lo), (others_out, 1 - z_lo)):
        total = got[0, z].astype(F32)
        for y in range(1, 4):
            total = total + got[y, z].astype(F32)
        out[...] = total.astype(out.dtype)


def add_chunks(place, got):
    part, n = got.shape[2:]
    shape = jax.ShapeDtypeStruct
    return pl.pallas_call(
        add_body,
        out_shape=[shape((part, n), F32), shape((part, n), BF16)],
        in_specs=[pl.BlockSpec(memory_space=pltpu.SMEM), VMEM],
        out_specs=[VMEM] * 2,
        compiler_params=pltpu.CompilerParams(vmem_limit_bytes=LIMIT),
        cost_estimate=SHORT,
        name="add_chunks",
    )(place, got)


def cores_body(keep, got, *refs):
    refs[-1][...] = (keep[...] + got[...].astype(F32)).astype(BF16)


def over_cores(send, keep, *after):
    got = other_core(send)
    part, n = keep.shape[2:]
    block = pl.BlockSpec((1, 2, part, n), lambda y: (y, 0, 0, 0))
    return pl.pallas_call(
        cores_body,
        grid=(4,),
        out_shape=jax.ShapeDtypeStruct(keep.shape, BF16),
        in_specs=[block, block] + [ANY] * len(after),
        out_specs=block,
        compiler_params=pltpu.CompilerParams(vmem_limit_bytes=LIMIT),
        cost_estimate=SHORT,
        name="over_cores",
    )(keep, got, *after)


def over_y(sums):
    groups = [[y * 4 + j for y in range(4)] for j in range(4)]
    return lax.all_to_all(sums, "dp", 0, 0, axis_index_groups=groups, tiled=True)


def over_rest(got, place):
    mine, others = add_chunks(place, got)
    return mine + other_z_lo(others).astype(F32)


def add_parts_body(groups, own, left, right, far, *refs):
    for g, out in enumerate(refs[-groups:]):
        total = own[g] + left[g].astype(F32) + right[g].astype(F32) + far[g].astype(F32)
        out[...] = total.astype(out.dtype)


def scatter_x(own, to_left, to_right, to_far, types, *after):
    got = along_x(to_left, -1), along_x(to_right, 1), along_x(to_far, 2)
    return pl.pallas_call(
        functools.partial(add_parts_body, len(types)),
        out_shape=[jax.ShapeDtypeStruct(own.shape[1:], kind) for kind in types],
        in_specs=[VMEM] * 4 + [ANY] * len(after),
        out_specs=[VMEM] * len(types),
        compiler_params=pltpu.CompilerParams(vmem_limit_bytes=LIMIT),
        cost_estimate=SHORT,
        name="add_parts",
    )(own, *got, *after)


def on_device(normed, out_grad, gate_weight, up_weight, down_weight):
    replicas = lax.axis_size("dp")
    dp = lax.axis_index("dp")
    place = jnp.stack((dp % 2, dp // 2 % 2)).astype(jnp.int32)
    weight = jnp.concatenate((gate_weight.T, up_weight.T), axis=0)
    own = jnp.stack((normed, out_grad))

    below, above = along_z(own, 1), along_z(own, -1)
    left, right = along_x(own, 1), along_x(own, -1)
    again = pack(normed, out_grad, left)
    home = [own, left, right, along_x(again, 2)]
    far = along_z(again, 2)
    b_left, b_right = along_x(below, 1), along_x(below, -1)
    a_left, a_right = along_x(above, 1), along_x(above, -1)
    b_far, a_far = along_x(b_left, 1), along_x(a_right, -1)
    near = [below, b_left, b_right, b_far, above, a_left, a_right, a_far]
    away = [far, along_x(far, 1), along_x(far, -1), along_x(far, 2)]

    home = stage(home, weight, down_weight, False)
    pair, down = weight_grad(place, home[0], home[2], None, False), weight_grad(place, home[1], home[3], None, False)
    near = stage(near, weight, down_weight, True)
    pair = weight_grad(place, near[0], near[2], pair[0], False)
    down = weight_grad(place, near[1], near[3], down[0], False)
    away = stage(away, weight, down_weight, False)
    pair = weight_grad(place, away[0], away[2], pair[0], True)
    late = late_partials([away[2], home[2]], weight, pair[0])
    pair = over_cores(*pair, late[0])
    down = weight_grad(place, away[1], away[3], down[0], True, pair)
    below, above = scatter_x(*near[4:], (BF16, BF16), down[0])
    from_below, from_above = along_z(above, 1), along_z(below, -1)
    pair = over_y(pair)
    down = over_cores(*down, pair)
    far, mine = scatter_x(*late, (BF16, F32), down, from_below, from_above)
    down = over_y(down)
    from_far = along_z(far, 2)
    grad_input = mine + from_below.astype(F32) + from_above.astype(F32) + from_far.astype(F32)

    grad_pair = over_rest(pair, place) / replicas
    grad_down = over_rest(down, place) / replicas
    half = gate_weight.shape[1]
    return grad_input.astype(BF16), grad_pair[:, :half], grad_pair[:, half:], grad_down.T


def solution(mesh):
    return jax.shard_map(
        on_device,
        mesh=mesh,
        in_specs=(
            P(("dp", "tensor"), None),
            P(("dp", "tensor"), None),
            P(None, "tensor"),
            P(None, "tensor"),
            P("tensor", None),
        ),
        out_specs=(
            P(("dp", "tensor"), None),
            P("dp", "tensor"),
            P("dp", "tensor"),
            P("tensor", "dp"),
        ),
        check_vma=False,
    )
```

```python
import functools

import jax
import jax.numpy as jnp
from jax import lax
from jax.experimental import pallas as pl
from jax.experimental.pallas import tpu as pltpu
from jax.sharding import PartitionSpec as P

F32, BF16 = jnp.float32, jnp.bfloat16
VMEM = pl.BlockSpec(memory_space=pltpu.VMEM)
ANY = pl.BlockSpec(memory_space=pl.ANY)
LIMIT = 40 << 20
SHORT = pl.CostEstimate(flops=0, bytes_accessed=0, transcendentals=0)


def contract(left, right, left_dim, right_dim):
    return lax.dot_general(
        left, right, (((left_dim,), (right_dim,)), ((), ())), preferred_element_type=F32
    )


def along_x(value, step):
    return lax.ppermute(value, "tensor", [(i, i // 4 * 4 + (i + step) % 4) for i in range(16)])


def along_z(value, step):
    return lax.ppermute(value, "tensor", [(i, (i + 4 * step) % 16) for i in range(16)])


def along_y(value, step):
    return lax.ppermute(value, "dp", [(i, (i + 4 * step) % 16) for i in range(16)])


def other_z_lo(value):
    return lax.ppermute(value, "dp", [(i, i ^ 2) for i in range(16)])


def other_core(value):
    return lax.ppermute(value, "dp", [(i, i ^ 1) for i in range(16)])


def pack_body(rows, grads, after, out):
    out[0], out[1] = rows[...], grads[...]


def pack(rows, grads, after):
    return pl.pallas_call(
        pack_body,
        out_shape=jax.ShapeDtypeStruct((2, *rows.shape), rows.dtype),
        in_specs=[VMEM, VMEM, ANY],
        out_specs=VMEM,
        cost_estimate=pl.CostEstimate(flops=0, bytes_accessed=1 << 20, transcendentals=0),
        name="pack",
    )(rows, grads, after)


def partials(both, weight, outs, g):
    tokens = outs[0].shape[1]
    grad = jnp.dot(both, weight[...], preferred_element_type=F32)
    outs[0][g] = grad[:tokens]
    for i in range(1, 4):
        outs[i][g] = grad[i * tokens : (i + 1) * tokens].astype(BF16)


def partial_shapes(groups, tokens, model):
    shape = jax.ShapeDtypeStruct
    return [shape((groups, tokens, model), F32)] + [shape((groups, tokens, model), BF16)] * 3


def stage_body(groups, send, *refs):
    blocks, (weight, down), outs = refs[: 4 * groups], refs[4 * groups : 4 * groups + 2], refs[4 * groups + 2 :]
    rows_out, grads_out, both_out, hidden_out = outs[:4]
    tokens, hidden_units = blocks[0].shape[1], down.shape[0]
    for i, block in enumerate(blocks):
        rows_out[i * tokens : (i + 1) * tokens, :] = block[0]
        grads_out[i * tokens : (i + 1) * tokens, :] = block[1]
    for g in range(groups):
        part_of = pl.ds(g * 4 * tokens, 4 * tokens)
        gate_up = contract(rows_out[part_of, :], weight[...], 1, 1)
        part = contract(grads_out[part_of, :], down[...], 1, 1)
        gate, up = gate_up[:, :hidden_units], gate_up[:, hidden_units:]
        sig = jax.nn.sigmoid(gate)
        act = gate * sig
        hidden_out[part_of, :] = (act * up).astype(BF16)
        dgate = (part * up * sig * (1.0 + gate * (1.0 - sig))).astype(BF16)
        dup = (part * act).astype(BF16)
        both = jnp.concatenate((dgate, dup), axis=1)
        both_out[part_of, :] = both
        if send:
            partials(both, weight, outs[4:], g)


def stage(blocks, weight, down, send):
    groups = len(blocks) // 4
    tokens, model = blocks[0].shape[1:]
    hidden_units = down.shape[0]
    m = len(blocks) * tokens
    shape = jax.ShapeDtypeStruct
    outs = [shape((m, model), BF16)] * 2 + [shape((m, 2 * hidden_units), BF16), shape((m, hidden_units), BF16)]
    if send:
        outs += partial_shapes(groups, tokens, model)
    return pl.pallas_call(
        functools.partial(stage_body, groups, send),
        out_shape=outs,
        in_specs=[VMEM] * (len(blocks) + 2),
        out_specs=[VMEM] * len(outs),
        compiler_params=pltpu.CompilerParams(vmem_limit_bytes=LIMIT),
        cost_estimate=SHORT if groups == 1 else pl.CostEstimate(
            flops=10 * m * model * hidden_units, bytes_accessed=groups * (6 << 20), transcendentals=m * hidden_units
        ),
        name="stage",
    )(*blocks, weight, down)


def late_body(groups, *refs):
    outs = refs[-4:]
    for g in range(groups):
        partials(refs[g][...], refs[groups], outs, g)


def late_partials(both, weight, *after):
    groups, m, model = len(both), both[0].shape[0], weight.shape[1]
    return pl.pallas_call(
        functools.partial(late_body, groups),
        out_shape=partial_shapes(groups, m // 4, model),
        in_specs=[VMEM] * (groups + 1) + [ANY] * len(after),
        out_specs=[VMEM] * 4,
        compiler_params=pltpu.CompilerParams(vmem_limit_bytes=LIMIT),
        cost_estimate=SHORT,
        name="late_partials",
    )(*both, weight, *after)


def weight_body(has_total, n_args, last, place, *refs):
    left, right = refs[0], refs[1]
    total = contract(left[...], right[...], 0, 0)
    if has_total:
        total = total + refs[2][...]
    outs = refs[n_args:]
    if not last:
        outs[0][...] = total
        return
    send, keep, held = outs
    core, part = place[0], keep.shape[2]
    held[...] = total
    for z in range(2):
        mine = pl.ds(pl.multiple_of(z * 2 * part + core * part, 32), part)
        others = pl.ds(pl.multiple_of(z * 2 * part + (1 - core) * part, 32), part)
        keep[0, z] = held[mine, :]
        send[0, z] = held[others, :].astype(BF16)


def weight_grad(place, left, right, total, last, after=None):
    m, model = left.shape
    n = right.shape[1]
    chunk, part = model // 4, model // 16
    shape = jax.ShapeDtypeStruct

    in_specs = [
        pl.BlockSpec((m, chunk), lambda r, place: (0, r)),
        pl.BlockSpec((m, n), lambda r, place: (0, 0)),
    ]
    args = [left, right]
    if total is not None:
        in_specs.append(pl.BlockSpec((chunk, n), lambda r, place: (r, 0)))
        args.append(total)
    if after is not None:
        in_specs.append(ANY)
        args.append(after)
    if last:
        out_specs = [pl.BlockSpec((1, 2, part, n), lambda r, place: (r, 0, 0, 0))] * 2
        out_shape = [shape((4, 2, part, n), BF16), shape((4, 2, part, n), F32)]
        scratch = [pltpu.VMEM((chunk, n), F32)]
    else:
        out_specs = [pl.BlockSpec((chunk, n), lambda r, place: (r, 0))]
        out_shape = [shape((model, n), F32)]
        scratch = []
    return pl.pallas_call(
        functools.partial(weight_body, total is not None, len(args), last),
        grid_spec=pltpu.PrefetchScalarGridSpec(
            num_scalar_prefetch=1, grid=(4,), in_specs=in_specs, out_specs=out_specs, scratch_shapes=scratch
        ),
        out_shape=out_shape,
        compiler_params=pltpu.CompilerParams(vmem_limit_bytes=LIMIT),
        cost_estimate=SHORT,
        name="weight_grad",
    )(place, *args)


def add_body(place, got, mine_out, others_out):
    z_lo = place[1]
    for out, z in ((mine_out, z_lo), (others_out, 1 - z_lo)):
        total = got[0, z].astype(F32)
        for y in range(1, 4):
            total = total + got[y, z].astype(F32)
        out[...] = total.astype(out.dtype)


def add_chunks(place, got):
    part, n = got.shape[2:]
    shape = jax.ShapeDtypeStruct
    return pl.pallas_call(
        add_body,
        out_shape=[shape((part, n), F32), shape((part, n), BF16)],
        in_specs=[pl.BlockSpec(memory_space=pltpu.SMEM), VMEM],
        out_specs=[VMEM] * 2,
        compiler_params=pltpu.CompilerParams(vmem_limit_bytes=LIMIT),
        cost_estimate=SHORT,
        name="add_chunks",
    )(place, got)


def cores_body(keep, got, *refs):
    refs[-1][...] = (keep[...] + got[...].astype(F32)).astype(BF16)


def over_cores(send, keep, *after):
    got = other_core(send)
    part, n = keep.shape[2:]
    block = pl.BlockSpec((1, 2, part, n), lambda y: (y, 0, 0, 0))
    return pl.pallas_call(
        cores_body,
        grid=(4,),
        out_shape=jax.ShapeDtypeStruct(keep.shape, BF16),
        in_specs=[block, block] + [ANY] * len(after),
        out_specs=block,
        compiler_params=pltpu.CompilerParams(vmem_limit_bytes=LIMIT),
        cost_estimate=SHORT,
        name="over_cores",
    )(keep, got, *after)


def over_y(sums):
    groups = [[y * 4 + j for y in range(4)] for j in range(4)]
    return lax.all_to_all(sums, "dp", 0, 0, axis_index_groups=groups, tiled=True)


def over_rest(got, place):
    mine, others = add_chunks(place, got)
    return mine + other_z_lo(others).astype(F32)


def add_parts_body(groups, own, left, right, far, *refs):
    for g, out in enumerate(refs[-groups:]):
        total = own[g] + left[g].astype(F32) + right[g].astype(F32) + far[g].astype(F32)
        out[...] = total.astype(out.dtype)


def scatter_x(own, to_left, to_right, to_far, types, *after):
    got = along_x(to_left, -1), along_x(to_right, 1), along_x(to_far, 2)
    return pl.pallas_call(
        functools.partial(add_parts_body, len(types)),
        out_shape=[jax.ShapeDtypeStruct(own.shape[1:], kind) for kind in types],
        in_specs=[VMEM] * 4 + [ANY] * len(after),
        out_specs=[VMEM] * len(types),
        compiler_params=pltpu.CompilerParams(vmem_limit_bytes=LIMIT),
        cost_estimate=SHORT,
        name="add_parts",
    )(own, *got, *after)


def on_device(normed, out_grad, gate_weight, up_weight, down_weight):
    replicas = lax.axis_size("dp")
    dp = lax.axis_index("dp")
    place = jnp.stack((dp % 2, dp // 2 % 2)).astype(jnp.int32)
    weight = jnp.concatenate((gate_weight.T, up_weight.T), axis=0)
    own = jnp.stack((normed, out_grad))

    below, above = along_z(own, 1), along_z(own, -1)
    left, right = along_x(own, 1), along_x(own, -1)
    again = pack(normed, out_grad, left)
    home = [own, left, right, along_x(again, 2)]
    far = along_z(again, 2)
    b_left, b_right = along_x(below, 1), along_x(below, -1)
    a_left, a_right = along_x(above, 1), along_x(above, -1)
    b_far, a_far = along_x(b_left, 1), along_x(a_right, -1)
    near = [below, b_left, b_right, b_far, above, a_left, a_right, a_far]
    away = [far, along_x(far, 1), along_x(far, -1), along_x(far, 2)]

    home = stage(home, weight, down_weight, False)
    pair, down = weight_grad(place, home[0], home[2], None, False), weight_grad(place, home[1], home[3], None, False)
    near = stage(near, weight, down_weight, True)
    pair = weight_grad(place, near[0], near[2], pair[0], False)
    down = weight_grad(place, near[1], near[3], down[0], False)
    away = stage(away, weight, down_weight, False)
    pair = weight_grad(place, away[0], away[2], pair[0], True)
    late = late_partials([away[2], home[2]], weight, pair[0])
    pair = over_cores(*pair, late[0])
    below, above = scatter_x(*near[4:], (BF16, BF16), pair)
    down = weight_grad(place, away[1], away[3], down[0], True, below)
    from_below, from_above = along_z(above, 1), along_z(below, -1)
    pair = over_y(pair)
    down = over_cores(*down, pair)
    far, mine = scatter_x(*late, (BF16, F32), down, from_below, from_above)
    down = over_y(down)
    from_far = along_z(far, 2)
    grad_input = mine + from_below.astype(F32) + from_above.astype(F32) + from_far.astype(F32)

    grad_pair = over_rest(pair, place) / replicas
    grad_down = over_rest(down, place) / replicas
    half = gate_weight.shape[1]
    return grad_input.astype(BF16), grad_pair[:, :half], grad_pair[:, half:], grad_down.T


def solution(mesh):
    return jax.shard_map(
        on_device,
        mesh=mesh,
        in_specs=(
            P(("dp", "tensor"), None),
            P(("dp", "tensor"), None),
            P(None, "tensor"),
            P(None, "tensor"),
            P("tensor", None),
        ),
        out_specs=(
            P(("dp", "tensor"), None),
            P("dp", "tensor"),
            P("dp", "tensor"),
            P("tensor", "dp"),
        ),
        check_vma=False,
    )
```

```python
import functools

import jax
import jax.numpy as jnp
from jax import lax
from jax.experimental import pallas as pl
from jax.experimental.pallas import tpu as pltpu
from jax.sharding import PartitionSpec as P

F32, BF16 = jnp.float32, jnp.bfloat16
VMEM = pl.BlockSpec(memory_space=pltpu.VMEM)
ANY = pl.BlockSpec(memory_space=pl.ANY)
LIMIT = 40 << 20
SHORT = pl.CostEstimate(flops=0, bytes_accessed=0, transcendentals=0)


def contract(left, right, left_dim, right_dim):
    return lax.dot_general(
        left, right, (((left_dim,), (right_dim,)), ((), ())), preferred_element_type=F32
    )


def along_x(value, step):
    return lax.ppermute(value, "tensor", [(i, i // 4 * 4 + (i + step) % 4) for i in range(16)])


def along_z(value, step):
    return lax.ppermute(value, "tensor", [(i, (i + 4 * step) % 16) for i in range(16)])


def along_y(value, step):
    return lax.ppermute(value, "dp", [(i, (i + 4 * step) % 16) for i in range(16)])


def other_z_lo(value):
    return lax.ppermute(value, "dp", [(i, i ^ 2) for i in range(16)])


def other_core(value):
    return lax.ppermute(value, "dp", [(i, i ^ 1) for i in range(16)])


def pack_body(rows, grads, after, out):
    out[0], out[1] = rows[...], grads[...]


def pack(rows, grads, after):
    return pl.pallas_call(
        pack_body,
        out_shape=jax.ShapeDtypeStruct((2, *rows.shape), rows.dtype),
        in_specs=[VMEM, VMEM, ANY],
        out_specs=VMEM,
        cost_estimate=pl.CostEstimate(flops=0, bytes_accessed=1 << 20, transcendentals=0),
        name="pack",
    )(rows, grads, after)


def partials(both, weight, outs, g):
    tokens = outs[0].shape[1]
    grad = jnp.dot(both, weight[...], preferred_element_type=F32)
    outs[0][g] = grad[:tokens]
    for i in range(1, 4):
        outs[i][g] = grad[i * tokens : (i + 1) * tokens].astype(BF16)


def partial_shapes(groups, tokens, model):
    shape = jax.ShapeDtypeStruct
    return [shape((groups, tokens, model), F32)] + [shape((groups, tokens, model), BF16)] * 3


def stage_body(groups, send, *refs):
    blocks, (weight, down), outs = refs[: 4 * groups], refs[4 * groups : 4 * groups + 2], refs[4 * groups + 2 :]
    rows_out, grads_out, both_out, hidden_out = outs[:4]
    tokens, hidden_units = blocks[0].shape[1], down.shape[0]
    for i, block in enumerate(blocks):
        rows_out[i * tokens : (i + 1) * tokens, :] = block[0]
        grads_out[i * tokens : (i + 1) * tokens, :] = block[1]
    for g in range(groups):
        part_of = pl.ds(g * 4 * tokens, 4 * tokens)
        gate_up = contract(rows_out[part_of, :], weight[...], 1, 1)
        part = contract(grads_out[part_of, :], down[...], 1, 1)
        gate, up = gate_up[:, :hidden_units], gate_up[:, hidden_units:]
        sig = jax.nn.sigmoid(gate)
        act = gate * sig
        hidden_out[part_of, :] = (act * up).astype(BF16)
        dgate = (part * up * sig * (1.0 + gate * (1.0 - sig))).astype(BF16)
        dup = (part * act).astype(BF16)
        both = jnp.concatenate((dgate, dup), axis=1)
        both_out[part_of, :] = both
        if send:
            partials(both, weight, outs[4:], g)


def stage(blocks, weight, down, send):
    groups = len(blocks) // 4
    tokens, model = blocks[0].shape[1:]
    hidden_units = down.shape[0]
    m = len(blocks) * tokens
    shape = jax.ShapeDtypeStruct
    outs = [shape((m, model), BF16)] * 2 + [shape((m, 2 * hidden_units), BF16), shape((m, hidden_units), BF16)]
    if send:
        outs += partial_shapes(groups, tokens, model)
    return pl.pallas_call(
        functools.partial(stage_body, groups, send),
        out_shape=outs,
        in_specs=[VMEM] * (len(blocks) + 2),
        out_specs=[VMEM] * len(outs),
        compiler_params=pltpu.CompilerParams(vmem_limit_bytes=LIMIT),
        cost_estimate=SHORT if groups == 1 else pl.CostEstimate(
            flops=10 * m * model * hidden_units, bytes_accessed=groups * (6 << 20), transcendentals=m * hidden_units
        ),
        name="stage",
    )(*blocks, weight, down)


def late_body(groups, *refs):
    outs = refs[-4:]
    for g in range(groups):
        partials(refs[g][...], refs[groups], outs, g)


def late_partials(both, weight, *after):
    groups, m, model = len(both), both[0].shape[0], weight.shape[1]
    return pl.pallas_call(
        functools.partial(late_body, groups),
        out_shape=partial_shapes(groups, m // 4, model),
        in_specs=[VMEM] * (groups + 1) + [ANY] * len(after),
        out_specs=[VMEM] * 4,
        compiler_params=pltpu.CompilerParams(vmem_limit_bytes=LIMIT),
        cost_estimate=SHORT,
        name="late_partials",
    )(*both, weight, *after)


def weight_body(has_total, n_args, last, place, *refs):
    left, right = refs[0], refs[1]
    total = contract(left[...], right[...], 0, 0)
    if has_total:
        total = total + refs[2][...]
    outs = refs[n_args:]
    if not last:
        outs[0][...] = total
        return
    send, keep, held = outs
    core, part = place[0], keep.shape[2]
    held[...] = total
    for z in range(2):
        mine = pl.ds(pl.multiple_of(z * 2 * part + core * part, 32), part)
        others = pl.ds(pl.multiple_of(z * 2 * part + (1 - core) * part, 32), part)
        keep[0, z] = held[mine, :]
        send[0, z] = held[others, :].astype(BF16)


def weight_grad(place, left, right, total, last, *after):
    m, model = left.shape
    n = right.shape[1]
    chunk, part = model // 4, model // 16
    shape = jax.ShapeDtypeStruct

    in_specs = [
        pl.BlockSpec((m, chunk), lambda r, place: (0, r)),
        pl.BlockSpec((m, n), lambda r, place: (0, 0)),
    ]
    args = [left, right]
    if total is not None:
        in_specs.append(pl.BlockSpec((chunk, n), lambda r, place: (r, 0)))
        args.append(total)
    in_specs += [ANY] * len(after)
    args += after
    if last:
        out_specs = [pl.BlockSpec((1, 2, part, n), lambda r, place: (r, 0, 0, 0))] * 2
        out_shape = [shape((4, 2, part, n), BF16), shape((4, 2, part, n), F32)]
        scratch = [pltpu.VMEM((chunk, n), F32)]
    else:
        out_specs = [pl.BlockSpec((chunk, n), lambda r, place: (r, 0))]
        out_shape = [shape((model, n), F32)]
        scratch = []
    return pl.pallas_call(
        functools.partial(weight_body, total is not None, len(args), last),
        grid_spec=pltpu.PrefetchScalarGridSpec(
            num_scalar_prefetch=1, grid=(4,), in_specs=in_specs, out_specs=out_specs, scratch_shapes=scratch
        ),
        out_shape=out_shape,
        compiler_params=pltpu.CompilerParams(vmem_limit_bytes=LIMIT),
        cost_estimate=SHORT,
        name="weight_grad",
    )(place, *args)


def add_body(place, got, mine_out, others_out):
    z_lo = place[1]
    for out, z in ((mine_out, z_lo), (others_out, 1 - z_lo)):
        total = got[0, z].astype(F32)
        for y in range(1, 4):
            total = total + got[y, z].astype(F32)
        out[...] = total.astype(out.dtype)


def add_chunks(place, got):
    part, n = got.shape[2:]
    shape = jax.ShapeDtypeStruct
    return pl.pallas_call(
        add_body,
        out_shape=[shape((part, n), F32), shape((part, n), BF16)],
        in_specs=[pl.BlockSpec(memory_space=pltpu.SMEM), VMEM],
        out_specs=[VMEM] * 2,
        compiler_params=pltpu.CompilerParams(vmem_limit_bytes=LIMIT),
        cost_estimate=SHORT,
        name="add_chunks",
    )(place, got)


def cores_body(keep, got, *refs):
    refs[-1][...] = (keep[...] + got[...].astype(F32)).astype(BF16)


def over_cores(send, keep, *after):
    got = other_core(send)
    part, n = keep.shape[2:]
    block = pl.BlockSpec((1, 2, part, n), lambda y: (y, 0, 0, 0))
    return pl.pallas_call(
        cores_body,
        grid=(4,),
        out_shape=jax.ShapeDtypeStruct(keep.shape, BF16),
        in_specs=[block, block] + [ANY] * len(after),
        out_specs=block,
        compiler_params=pltpu.CompilerParams(vmem_limit_bytes=LIMIT),
        cost_estimate=SHORT,
        name="over_cores",
    )(keep, got, *after)


def over_y(sums):
    groups = [[y * 4 + j for y in range(4)] for j in range(4)]
    return lax.all_to_all(sums, "dp", 0, 0, axis_index_groups=groups, tiled=True)


def over_rest(got, place):
    mine, others = add_chunks(place, got)
    return mine + other_z_lo(others).astype(F32)


def add_parts_body(first, groups, own, left, right, far, *refs):
    for g, out in enumerate(refs[-groups:], first):
        total = own[g] + left[g].astype(F32) + right[g].astype(F32) + far[g].astype(F32)
        out[...] = total.astype(out.dtype)


def exchange_x(own, to_left, to_right, to_far):
    return own, along_x(to_left, -1), along_x(to_right, 1), along_x(to_far, 2)


def add_parts(own, left, right, far, first, types, *after):
    return pl.pallas_call(
        functools.partial(add_parts_body, first, len(types)),
        out_shape=[jax.ShapeDtypeStruct(own.shape[1:], kind) for kind in types],
        in_specs=[VMEM] * 4 + [ANY] * len(after),
        out_specs=[VMEM] * len(types),
        compiler_params=pltpu.CompilerParams(vmem_limit_bytes=LIMIT),
        cost_estimate=SHORT,
        name="add_parts",
    )(own, left, right, far, *after)


def on_device(normed, out_grad, gate_weight, up_weight, down_weight):
    replicas = lax.axis_size("dp")
    dp = lax.axis_index("dp")
    place = jnp.stack((dp % 2, dp // 2 % 2)).astype(jnp.int32)
    weight = jnp.concatenate((gate_weight.T, up_weight.T), axis=0)
    own = jnp.stack((normed, out_grad))

    below, above = along_z(own, 1), along_z(own, -1)
    left, right = along_x(own, 1), along_x(own, -1)
    again = pack(normed, out_grad, left)
    home = [own, left, right, along_x(again, 2)]
    far = along_z(again, 2)
    b_left, b_right = along_x(below, 1), along_x(below, -1)
    a_left, a_right = along_x(above, 1), along_x(above, -1)
    b_far, a_far = along_x(b_left, 1), along_x(a_right, -1)
    near = [below, b_left, b_right, b_far, above, a_left, a_right, a_far]
    away = [far, along_x(far, 1), along_x(far, -1), along_x(far, 2)]

    home = stage(home, weight, down_weight, False)
    pair, down = weight_grad(place, home[0], home[2], None, False), weight_grad(place, home[1], home[3], None, False)
    near = stage(near, weight, down_weight, True)
    pair = weight_grad(place, near[0], near[2], pair[0], False)
    down = weight_grad(place, near[1], near[3], down[0], False)
    away = stage(away, weight, down_weight, False)
    pair = weight_grad(place, away[0], away[2], pair[0], True)
    pair = over_cores(*pair)
    late = late_partials([away[2], home[2]], weight, pair)
    near = exchange_x(*near[4:])
    below, above = add_parts(*near, 0, (BF16, BF16), late[0])
    down = weight_grad(place, away[1], away[3], down[0], True, late[0], *near[1:])
    pair = over_y(pair)
    parts = exchange_x(*late)
    down = over_cores(*down, pair, parts[1])
    from_below, from_above = along_z(above, 1), along_z(below, -1)
    far, mine = add_parts(*parts, 0, (BF16, F32), down, from_below, from_above)
    down = over_y(down)
    from_far = along_z(far, 2)
    grad_input = mine + from_below.astype(F32) + from_above.astype(F32) + from_far.astype(F32)

    grad_pair = over_rest(pair, place) / replicas
    grad_down = over_rest(down, place) / replicas
    half = gate_weight.shape[1]
    return grad_input.astype(BF16), grad_pair[:, :half], grad_pair[:, half:], grad_down.T


def solution(mesh):
    return jax.shard_map(
        on_device,
        mesh=mesh,
        in_specs=(
            P(("dp", "tensor"), None),
            P(("dp", "tensor"), None),
            P(None, "tensor"),
            P(None, "tensor"),
            P("tensor", None),
        ),
        out_specs=(
            P(("dp", "tensor"), None),
            P("dp", "tensor"),
            P("dp", "tensor"),
            P("tensor", "dp"),
        ),
        check_vma=False,
    )
```

```python
import functools

import jax
import jax.numpy as jnp
from jax import lax
from jax.experimental import pallas as pl
from jax.experimental.pallas import tpu as pltpu
from jax.sharding import PartitionSpec as P

F32, BF16 = jnp.float32, jnp.bfloat16
VMEM = pl.BlockSpec(memory_space=pltpu.VMEM)
ANY = pl.BlockSpec(memory_space=pl.ANY)
LIMIT = 40 << 20
SHORT = pl.CostEstimate(flops=0, bytes_accessed=0, transcendentals=0)


def contract(left, right, left_dim, right_dim):
    return lax.dot_general(
        left, right, (((left_dim,), (right_dim,)), ((), ())), preferred_element_type=F32
    )


def along_x(value, step):
    return lax.ppermute(value, "tensor", [(i, i // 4 * 4 + (i + step) % 4) for i in range(16)])


def along_z(value, step):
    return lax.ppermute(value, "tensor", [(i, (i + 4 * step) % 16) for i in range(16)])


def along_y(value, step):
    return lax.ppermute(value, "dp", [(i, (i + 4 * step) % 16) for i in range(16)])


def other_z_lo(value):
    return lax.ppermute(value, "dp", [(i, i ^ 2) for i in range(16)])


def other_core(value):
    return lax.ppermute(value, "dp", [(i, i ^ 1) for i in range(16)])


def pack_body(rows, grads, after, out):
    out[0], out[1] = rows[...], grads[...]


def pack(rows, grads, after):
    return pl.pallas_call(
        pack_body,
        out_shape=jax.ShapeDtypeStruct((2, *rows.shape), rows.dtype),
        in_specs=[VMEM, VMEM, ANY],
        out_specs=VMEM,
        cost_estimate=pl.CostEstimate(flops=0, bytes_accessed=1 << 20, transcendentals=0),
        name="pack",
    )(rows, grads, after)


def partials(both, weight, outs, g):
    tokens = outs[0].shape[1]
    grad = jnp.dot(both, weight[...], preferred_element_type=F32)
    outs[0][g] = grad[:tokens]
    for i in range(1, 4):
        outs[i][g] = grad[i * tokens : (i + 1) * tokens].astype(BF16)


def partial_shapes(groups, tokens, model):
    shape = jax.ShapeDtypeStruct
    return [shape((groups, tokens, model), F32)] + [shape((groups, tokens, model), BF16)] * 3


def stage_body(groups, send, *refs):
    blocks, (weight, down), outs = refs[: 4 * groups], refs[4 * groups : 4 * groups + 2], refs[4 * groups + 2 :]
    rows_out, grads_out, both_out, hidden_out = outs[:4]
    tokens, hidden_units = blocks[0].shape[1], down.shape[0]
    for i, block in enumerate(blocks):
        rows_out[i * tokens : (i + 1) * tokens, :] = block[0]
        grads_out[i * tokens : (i + 1) * tokens, :] = block[1]
    for g in range(groups):
        part_of = pl.ds(g * 4 * tokens, 4 * tokens)
        gate_up = contract(rows_out[part_of, :], weight[...], 1, 1)
        part = contract(grads_out[part_of, :], down[...], 1, 1)
        gate, up = gate_up[:, :hidden_units], gate_up[:, hidden_units:]
        sig = jax.nn.sigmoid(gate)
        act = gate * sig
        hidden_out[part_of, :] = (act * up).astype(BF16)
        dgate = (part * up * sig * (1.0 + gate * (1.0 - sig))).astype(BF16)
        dup = (part * act).astype(BF16)
        both = jnp.concatenate((dgate, dup), axis=1)
        both_out[part_of, :] = both
        if send:
            partials(both, weight, outs[4:], g)


def stage(blocks, weight, down, send):
    groups = len(blocks) // 4
    tokens, model = blocks[0].shape[1:]
    hidden_units = down.shape[0]
    m = len(blocks) * tokens
    shape = jax.ShapeDtypeStruct
    outs = [shape((m, model), BF16)] * 2 + [shape((m, 2 * hidden_units), BF16), shape((m, hidden_units), BF16)]
    if send:
        outs += partial_shapes(groups, tokens, model)
    return pl.pallas_call(
        functools.partial(stage_body, groups, send),
        out_shape=outs,
        in_specs=[VMEM] * (len(blocks) + 2),
        out_specs=[VMEM] * len(outs),
        compiler_params=pltpu.CompilerParams(vmem_limit_bytes=LIMIT),
        cost_estimate=SHORT if groups == 1 else pl.CostEstimate(
            flops=10 * m * model * hidden_units, bytes_accessed=groups * (6 << 20), transcendentals=m * hidden_units
        ),
        name="stage",
    )(*blocks, weight, down)


def late_body(groups, *refs):
    outs = refs[-4:]
    for g in range(groups):
        partials(refs[g][...], refs[groups], outs, g)


def late_partials(both, weight, *after):
    groups, m, model = len(both), both[0].shape[0], weight.shape[1]
    return pl.pallas_call(
        functools.partial(late_body, groups),
        out_shape=partial_shapes(groups, m // 4, model),
        in_specs=[VMEM] * (groups + 1) + [ANY] * len(after),
        out_specs=[VMEM] * 4,
        compiler_params=pltpu.CompilerParams(vmem_limit_bytes=LIMIT),
        cost_estimate=SHORT,
        name="late_partials",
    )(*both, weight, *after)


def weight_body(has_total, n_args, last, place, *refs):
    left, right = refs[0], refs[1]
    total = contract(left[...], right[...], 0, 0)
    if has_total:
        total = total + refs[2][...]
    outs = refs[n_args:]
    if not last:
        outs[0][...] = total
        return
    send, keep, held = outs
    core, part = place[0], keep.shape[2]
    held[...] = total
    for z in range(2):
        mine = pl.ds(pl.multiple_of(z * 2 * part + core * part, 32), part)
        others = pl.ds(pl.multiple_of(z * 2 * part + (1 - core) * part, 32), part)
        keep[0, z] = held[mine, :]
        send[0, z] = held[others, :].astype(BF16)


def weight_grad(place, left, right, total, last, *after):
    m, model = left.shape
    n = right.shape[1]
    chunk, part = model // 4, model // 16
    shape = jax.ShapeDtypeStruct

    in_specs = [
        pl.BlockSpec((m, chunk), lambda r, place: (0, r)),
        pl.BlockSpec((m, n), lambda r, place: (0, 0)),
    ]
    args = [left, right]
    if total is not None:
        in_specs.append(pl.BlockSpec((chunk, n), lambda r, place: (r, 0)))
        args.append(total)
    in_specs += [ANY] * len(after)
    args += after
    if last:
        out_specs = [pl.BlockSpec((1, 2, part, n), lambda r, place: (r, 0, 0, 0))] * 2
        out_shape = [shape((4, 2, part, n), BF16), shape((4, 2, part, n), F32)]
        scratch = [pltpu.VMEM((chunk, n), F32)]
    else:
        out_specs = [pl.BlockSpec((chunk, n), lambda r, place: (r, 0))]
        out_shape = [shape((model, n), F32)]
        scratch = []
    return pl.pallas_call(
        functools.partial(weight_body, total is not None, len(args), last),
        grid_spec=pltpu.PrefetchScalarGridSpec(
            num_scalar_prefetch=1, grid=(4,), in_specs=in_specs, out_specs=out_specs, scratch_shapes=scratch
        ),
        out_shape=out_shape,
        compiler_params=pltpu.CompilerParams(vmem_limit_bytes=LIMIT),
        cost_estimate=SHORT,
        name="weight_grad",
    )(place, *args)


def add_body(place, got, mine_out, others_out):
    z_lo = place[1]
    for out, z in ((mine_out, z_lo), (others_out, 1 - z_lo)):
        total = got[0, z].astype(F32)
        for y in range(1, 4):
            total = total + got[y, z].astype(F32)
        out[...] = total.astype(out.dtype)


def add_chunks(place, got):
    part, n = got.shape[2:]
    shape = jax.ShapeDtypeStruct
    return pl.pallas_call(
        add_body,
        out_shape=[shape((part, n), F32), shape((part, n), BF16)],
        in_specs=[pl.BlockSpec(memory_space=pltpu.SMEM), VMEM],
        out_specs=[VMEM] * 2,
        compiler_params=pltpu.CompilerParams(vmem_limit_bytes=LIMIT),
        cost_estimate=SHORT,
        name="add_chunks",
    )(place, got)


def cores_body(keep, got, *refs):
    refs[-1][...] = (keep[...] + got[...].astype(F32)).astype(BF16)


def over_cores(send, keep, *after):
    got = other_core(send)
    part, n = keep.shape[2:]
    block = pl.BlockSpec((1, 2, part, n), lambda y: (y, 0, 0, 0))
    return pl.pallas_call(
        cores_body,
        grid=(4,),
        out_shape=jax.ShapeDtypeStruct(keep.shape, BF16),
        in_specs=[block, block] + [ANY] * len(after),
        out_specs=block,
        compiler_params=pltpu.CompilerParams(vmem_limit_bytes=LIMIT),
        cost_estimate=SHORT,
        name="over_cores",
    )(keep, got, *after)


def over_y(sums):
    groups = [[y * 4 + j for y in range(4)] for j in range(4)]
    return lax.all_to_all(sums, "dp", 0, 0, axis_index_groups=groups, tiled=True)


def over_rest(got, place):
    mine, others = add_chunks(place, got)
    return mine + other_z_lo(others).astype(F32)


def add_parts_body(first, groups, own, left, right, far, *refs):
    for g, out in enumerate(refs[-groups:], first):
        total = own[g] + left[g].astype(F32) + right[g].astype(F32) + far[g].astype(F32)
        out[...] = total.astype(out.dtype)


def exchange_x(own, to_left, to_right, to_far):
    return own, along_x(to_left, -1), along_x(to_right, 1), along_x(to_far, 2)


def add_parts(own, left, right, far, first, types, *after):
    return pl.pallas_call(
        functools.partial(add_parts_body, first, len(types)),
        out_shape=[jax.ShapeDtypeStruct(own.shape[1:], kind) for kind in types],
        in_specs=[VMEM] * 4 + [ANY] * len(after),
        out_specs=[VMEM] * len(types),
        compiler_params=pltpu.CompilerParams(vmem_limit_bytes=LIMIT),
        cost_estimate=SHORT,
        name="add_parts",
    )(own, left, right, far, *after)


def on_device(normed, out_grad, gate_weight, up_weight, down_weight):
    replicas = lax.axis_size("dp")
    dp = lax.axis_index("dp")
    place = jnp.stack((dp % 2, dp // 2 % 2)).astype(jnp.int32)
    weight = jnp.concatenate((gate_weight.T, up_weight.T), axis=0)
    own = jnp.stack((normed, out_grad))

    below, above = along_z(own, 1), along_z(own, -1)
    left, right = along_x(own, 1), along_x(own, -1)
    again = pack(normed, out_grad, left)
    home = [own, left, right, along_x(again, 2)]
    far = along_z(again, 2)
    b_left, b_right = along_x(below, 1), along_x(below, -1)
    a_left, a_right = along_x(above, 1), along_x(above, -1)
    b_far, a_far = along_x(b_left, 1), along_x(a_right, -1)
    near = [below, b_left, b_right, b_far, above, a_left, a_right, a_far]
    away = [far, along_x(far, 1), along_x(far, -1), along_x(far, 2)]

    home = stage(home, weight, down_weight, False)
    pair, down = weight_grad(place, home[0], home[2], None, False), weight_grad(place, home[1], home[3], None, False)
    near = stage(near, weight, down_weight, True)
    pair = weight_grad(place, near[0], near[2], pair[0], False)
    down = weight_grad(place, near[1], near[3], down[0], False)
    away = stage(away, weight, down_weight, False)
    pair = weight_grad(place, away[0], away[2], pair[0], True)
    pair = over_cores(*pair)
    late = late_partials([away[2], home[2]], weight, pair)
    near = exchange_x(*near[4:])
    down = weight_grad(place, away[1], away[3], down[0], True, late[0], *near[1:])
    pair = over_y(pair)
    parts = exchange_x(*late)
    down = over_cores(*down, pair, parts[1])
    below, above = add_parts(*near, 0, (BF16, BF16), down)
    from_below, from_above = along_z(above, 1), along_z(below, -1)
    far, mine = add_parts(*parts, 0, (BF16, F32), below)
    down = over_y(down)
    from_far = along_z(far, 2)
    grad_input = mine + from_below.astype(F32) + from_above.astype(F32) + from_far.astype(F32)

    grad_pair = over_rest(pair, place) / replicas
    grad_down = over_rest(down, place) / replicas
    half = gate_weight.shape[1]
    return grad_input.astype(BF16), grad_pair[:, :half], grad_pair[:, half:], grad_down.T


def solution(mesh):
    return jax.shard_map(
        on_device,
        mesh=mesh,
        in_specs=(
            P(("dp", "tensor"), None),
            P(("dp", "tensor"), None),
            P(None, "tensor"),
            P(None, "tensor"),
            P("tensor", None),
        ),
        out_specs=(
            P(("dp", "tensor"), None),
            P("dp", "tensor"),
            P("dp", "tensor"),
            P("tensor", "dp"),
        ),
        check_vma=False,
    )
```
